32 devices in a mesh: slab: 8 (over y, x, core), tile: 4 (over z).
Axes of the slice: x: 2, y: 2, z: 4, core: 2. Of those that a mesh axis runs over, the one named last changes fastest.
Arguments:
- field: float32 [64, 64, 1024], P('slab', 'tile'), may hold values from -1 to 1
- dual: float32 [3, 64, 64, 1024], P(None, 'slab', 'tile'), may hold values from -0.5 to 0.5
- depth: float32 [8, 2, 4, 64, 1024], P('slab', None, None, 'tile'), may hold values from 0 to 64
- owner: int32 [2], replicated, may hold values from 0 to 7
- visible: int32 [2, 4, 4], P(None, None, 'tile'), may hold values 0 or 1
Outputs:
- field_out: float32 [64, 64, 1024], P('slab', 'tile')
- dual_out: float32 [3, 64, 64, 1024], P(None, 'slab', 'tile')
The draws below stay inside these ranges and needn't reach their ends.
All inputs are finite; a program needn't handle non-finite values. No bound on the sum of `visible` on one device may be relied on, other than what follows from the above.
Results may differ from the reference program's by a relative error of at most 0.00002.
Values sent between devices are 32-bit elements; how exact they have to be, the bound alone decides.
A program may use at most 64 MiB of HBM per device.

```python
import jax
import jax.numpy as jnp

CX = 16
NY = 1024
VIEWS = 4
BINS = 8
BAND = 6
ITERS = 2
NZ = 64
NX = 64
N_SLAB = 8
N_TILE = 4


def touch_ends(array, key, low, largest):
    shape = array.shape
    spot = [jax.random.randint(jax.random.fold_in(key, axis), (), 0, shape[axis]) for axis in range(len(shape))]
    array = array.at[tuple(spot)].set(low)
    longest = shape.index(max(shape))
    spot[longest] = (spot[longest] + 1) % shape[longest]
    return array.at[tuple(spot)].set(largest)


def block_scale(own_key, dims, pieces, least, top_value):
    gain = 1.0
    for position, parts in pieces:
        draws = jax.random.uniform(jax.random.fold_in(jax.random.fold_in(own_key, 6), position), (parts,), jnp.float32, least / len(pieces), top_value / len(pieces))
        gain = gain * jnp.repeat(jnp.exp(draws), dims[position] // parts).reshape((-1,) + (1,) * (len(dims) - 1 - position))
    return gain


def setup_inputs(seed: int = 0) -> dict:
    key_list = jax.random.split(jax.random.key(seed), 6)
    field = jnp.clip(jax.random.uniform(key_list[0], (NZ, NX, NY), jnp.float32, -1.0, 1.0) * block_scale(key_list[0], (NZ, NX, NY), ((0, 8), (1, 4)), -0.4, 0.0), -1.0, 1.0)
    dual = jnp.clip(jax.random.uniform(key_list[1], (3, NZ, NX, NY), jnp.float32, -0.5, 0.5) * block_scale(key_list[1], (3, NZ, NX, NY), ((1, 8), (2, 4)), -0.4, 0.0), -0.5, 0.5)
    depth = jnp.clip(64.0 * jax.random.uniform(key_list[2], (N_SLAB, ITERS, VIEWS, NX, NY), jnp.float32) ** block_scale(key_list[2], (N_SLAB, ITERS, VIEWS, NX, NY), ((0, 8), (3, 4)), -0.2, 0.2), 0.0, 64.0)
    owner = jax.random.randint(key_list[3], (ITERS,), 0, N_SLAB).astype(jnp.int32)
    visible = touch_ends((jax.random.randint(key_list[4], (ITERS, VIEWS, N_TILE), 0, 4) < 3).astype(jnp.int32), jax.random.fold_in(key_list[4], 1), 0, 1)
    return dict(field=field, dual=dual, depth=depth, owner=owner, visible=visible)


def add_votes(histogram, depth_map, seen, zpos):
    ratio = (depth_map[None, :, :] - zpos) / float(BAND)
    weight = jnp.clip(ratio + 2.0, 0.0, 1.0) * seen
    place = (jnp.clip(ratio, -1.0, 1.0) + 1.0) * ((BINS - 1) / 2.0)
    return [histogram[bin_index] + weight * jnp.maximum(0.0, 1.0 - jnp.abs(place - float(bin_index))) for bin_index in range(BINS)]

def proximal(values, histogram):
    total = histogram[0]
    for bin_index in range(1, BINS):
        total = total + histogram[bin_index]
    weights = -total
    best = jnp.minimum(values - 0.05 * weights, -1.0)
    weights = weights + 2.0 * histogram[0]
    for bin_index in range(1, BINS):
        centre = -1.0 + 2.0 * bin_index / (BINS - 1)
        best = jnp.maximum(best, jnp.minimum(values - 0.05 * weights, centre))
        weights = weights + 2.0 * histogram[bin_index]
    return jnp.maximum(best, values - 0.05 * weights)

def reference(field, dual, depth, owner, visible):
    zpos = jnp.arange(NZ, dtype=jnp.int32)[:, None, None]
    xpos = jnp.arange(NX, dtype=jnp.int32)[None, :, None]
    ypos = jnp.arange(NY, dtype=jnp.int32)[None, None, :]
    zfloat = zpos.astype(jnp.float32)
    strip = jnp.arange(NX, dtype=jnp.int32) // CX
    histogram = [jnp.zeros((NZ, NX, NY), jnp.float32) for bin_index in range(BINS)]
    current = field
    dual_z, dual_x, dual_y = (dual[0], dual[1], dual[2])
    extra = field
    for step_index in range(ITERS):
        for view_index in range(VIEWS):
            depth_map = depth[owner[step_index], step_index, view_index]
            seen = visible[step_index, view_index][strip].astype(jnp.float32)[None, :, None]
            histogram = add_votes(histogram, depth_map, seen, zfloat)
        zero_z = jnp.zeros((1, NX, NY), jnp.float32)
        zero_x = jnp.zeros((NZ, 1, NY), jnp.float32)
        zero_y = jnp.zeros((NZ, NX, 1), jnp.float32)
        grad_z = jnp.where(zpos < NZ - 1, jnp.concatenate([extra[1:], zero_z], 0) - extra, 0.0)
        grad_x = jnp.where(xpos < NX - 1, jnp.concatenate([extra[:, 1:], zero_x], 1) - extra, 0.0)
        grad_y = jnp.where(ypos < NY - 1, jnp.concatenate([extra[:, :, 1:], zero_y], 2) - extra, 0.0)
        moved_z = dual_z + 0.25 * grad_z
        moved_x = dual_x + 0.25 * grad_x
        moved_y = dual_y + 0.25 * grad_y
        scale = jnp.maximum(1.0, jnp.sqrt(moved_z * moved_z + moved_x * moved_x + moved_y * moved_y))
        dual_z = jnp.where(zpos < NZ - 1, moved_z / scale, 0.0)
        dual_x = jnp.where(xpos < NX - 1, moved_x / scale, 0.0)
        dual_y = jnp.where(ypos < NY - 1, moved_y / scale, 0.0)
        prev_z = jnp.concatenate([zero_z, dual_z[:-1]], 0)
        prev_x = jnp.concatenate([zero_x, dual_x[:, :-1]], 1)
        prev_y = jnp.concatenate([zero_y, dual_y[:, :, :-1]], 2)
        divergence = dual_z - prev_z + (dual_x - prev_x) + (dual_y - prev_y)
        updated = proximal(current + 0.25 * divergence, histogram)
        extra = 2.0 * updated - current
        current = updated
    return (current, jnp.stack([dual_z, dual_x, dual_y]))
```

```python
import functools

import jax
import jax.numpy as jnp
from jax import lax
from jax.experimental import pallas as pl
from jax.experimental.pallas import tpu as pltpu
from jax.sharding import PartitionSpec as P

VIEWS = 4
BINS = 8
BAND = 6
ITERS = 2

ROWS = 8
UNIT = 0.35
HALF = VIEWS // 2
MESH = pl.DeviceIdType.MESH


def kernel(
    n_slab,
    n_tile,
    owner_ref,
    visible_ref,
    field_ref,
    dual_ref,
    depth_ref,
    field_out,
    dual_out,
    extra,
    start_p,
    dual_z,
    dual_x,
    dual_y,
    part,
    value,
    votes,
    mine,
    got,
    kept,
    batch,
    row_send,
    row_recv,
    depth_send,
    depth_recv,
    halo_send,
    halo_recv,
    local_sem,
):
    nz, nx, ny = field_ref.shape
    groups = nx // ROWS
    chunk = min(256, ny)
    chunks = ny // chunk
    slab = lax.axis_index("slab")
    tile = lax.axis_index("tile")
    bits = []
    while 2 ** len(bits) < n_slab:
        bits.append(len(bits))
    middle = bits[1:]
    order = (middle, middle[::-1])
    last = len(middle) + 1
    side = [lax.rem(lax.div(slab, 2**b), 2) for b in bits]
    partner = [slab + 2**b * (1 - 2 * side[b]) for b in bits]
    core = side[0]
    first_slab, last_slab = slab == 0, slab == n_slab - 1
    first_tile, last_tile = tile == 0, tile == n_tile - 1

    into_field = pltpu.make_async_copy(
        field_ref, extra.at[0, pl.ds(0, nz), pl.ds(0, nx)], local_sem.at[0]
    )
    into_dual = pltpu.make_async_copy(dual_ref, start_p, local_sem.at[1])
    into_mine = [
        pltpu.make_async_copy(
            depth_ref.at[0, k, pl.ds(HALF * core, HALF)], mine.at[k], local_sem.at[2 + k]
        )
        for k in range(ITERS)
    ]
    into_field.start()
    into_mine[0].start()
    into_mine[1].start()
    into_dual.start()

    barrier = pltpu.get_barrier_semaphore()
    for b in bits:
        pl.semaphore_signal(
            barrier, inc=1, device_id={"slab": partner[b]}, device_id_type=MESH
        )
    greeted = len(bits)
    for axis, place, here, there in (
        ("slab", slab, first_slab, -1),
        ("slab", slab, last_slab, 1),
        ("tile", tile, first_tile, -1),
        ("tile", tile, last_tile, 1),
    ):

        @pl.when(jnp.logical_not(here))
        def _(axis=axis, place=place, there=there):
            pl.semaphore_signal(
                barrier, inc=1, device_id={axis: place + there}, device_id_type=MESH
            )

    inner = [jnp.where(edge, 0, 1) for edge in (first_slab, last_slab, first_tile, last_tile)]
    pl.semaphore_wait(barrier, greeted + inner[0] + inner[1] + inner[2] + inner[3])

    def exchange(k, stage, piece, source, target, b):
        return pltpu.make_async_remote_copy(
            src_ref=source,
            dst_ref=target,
            send_sem=depth_send.at[k, stage, piece],
            recv_sem=depth_recv.at[k, stage, piece],
            device_id={"slab": partner[b]},
            device_id_type=MESH,
        )

    def first_copy(k):
        return exchange(
            k,
            0,
            0,
            depth_ref.at[0, k, pl.ds(HALF * (1 - core), HALF)],
            got.at[k, 0],
            0,
        )

    def middle_copy(k, stage, piece):
        return exchange(
            k,
            stage,
            piece,
            kept.at[k, stage - 1, piece],
            got.at[k, stage, piece],
            order[piece][stage - 1],
        )

    def last_copy(k):
        there = batch.at[k, pl.ds(HALF * core, HALF)]
        return exchange(k, last, 0, there, there, 0)

    def owned(k, b):
        return lax.rem(lax.div(owner_ref[k], 2**b), 2) == side[b]

    def scaled(k, piece, depth):
        seen = jnp.where(core == 0, visible_ref[k, piece, 0], visible_ref[k, HALF + piece, 0])
        return jnp.where(seen == 1, depth * (UNIT / BAND) + 2.0 * UNIT, -1e6)

    def keep(k, stage, piece, chosen):
        if stage < last - 1:
            kept[k, stage, piece] = chosen
        else:
            batch[k, HALF * core + piece] = scaled(k, piece, chosen)

    def forward(k, stage, piece):
        if stage == 0:
            keep(k, 0, piece, jnp.where(owned(k, 0), mine[k, piece], got[k, 0, piece]))
        else:
            b = order[piece][stage - 1]
            keep(
                k,
                stage,
                piece,
                jnp.where(owned(k, b), kept[k, stage - 1, piece], got[k, stage, piece]),
            )

    def pass_on(k, stage):
        if stage == 0:
            into_mine[k].wait()
            first_copy(k).wait_recv()
        for piece in range(2):
            if stage > 0:
                middle_copy(k, stage, piece).wait_recv()
            forward(k, stage, piece)
            if stage < last - 1:
                middle_copy(k, stage + 1, piece).start()
        if stage == last - 1:
            last_copy(k).start()

    def halo(it, kind):
        if kind == 0:
            source, target = extra.at[it, 0, pl.ds(0, nx)], extra.at[it, nz, pl.ds(0, nx)]
            device = {"slab": slab - 1}
        elif kind == 1:
            source, target = row_send.at[it, 0], row_recv.at[it, 0]
            device = {"tile": tile - 1}
        elif kind == 2:
            source, target = dual_z.at[it, nz], dual_z.at[it, 0]
            device = {"slab": slab + 1}
        else:
            source, target = row_send.at[it, 1], row_recv.at[it, 1]
            device = {"tile": tile + 1}
        return pltpu.make_async_remote_copy(
            src_ref=source,
            dst_ref=target,
            send_sem=halo_send.at[it, kind],
            recv_sem=halo_recv.at[it, kind],
            device_id=device,
            device_id_type=MESH,
        )

    sends_not = (first_slab, first_tile, last_slab, last_tile)
    gets_not = (last_slab, last_tile, first_slab, first_tile)

    def send_halo(it, kind):
        @pl.when(jnp.logical_not(sends_not[kind]))
        def _():
            halo(it, kind).start()

    def sent_halo(it, kind):
        @pl.when(jnp.logical_not(sends_not[kind]))
        def _():
            halo(it, kind).wait_send()

    def take_halo(it, kind):
        @pl.when(jnp.logical_not(gets_not[kind]))
        def _():
            halo(it, kind).wait_recv()
            for z in range(nz):
                if kind == 1:
                    extra[it, z, nx : nx + 1, :] = row_recv[it, 0, z : z + 1, :]
                if kind == 3:
                    dual_x[it, z, ROWS - 1 : ROWS, :] = row_recv[it, 1, z : z + 1, :]

        @pl.when(gets_not[kind])
        def _():
            if kind == 0:
                extra[it, nz, 0:nx, :] = jnp.zeros((nx, ny), jnp.float32)
            if kind == 2:
                dual_z[it, 0] = jnp.zeros((nx, ny), jnp.float32)
            for z in range(nz):
                if kind == 1:
                    extra[it, z, nx : nx + 1, :] = jnp.zeros((1, ny), jnp.float32)
                if kind == 3:
                    dual_x[it, z, ROWS - 1 : ROWS, :] = jnp.zeros((1, ny), jnp.float32)

    def pack_extra(it):
        for z in range(nz):
            row_send[it, 0, z : z + 1, :] = extra[it, z, 0:1, :]

    def pack_dual(it):
        for z in range(nz):
            row_send[it, 1, z : z + 1, :] = dual_x[it, z, ROWS + nx - 1 : ROWS + nx, :]

    def dual_pass(it, group, low, high):
        row = ROWS * group
        lane = lax.broadcasted_iota(jnp.int32, (ROWS, ny), 1)
        inside_y = jnp.where(lane < ny - 1, 1.0, 0.0)
        rows = lax.broadcasted_iota(jnp.int32, (ROWS, ny), 0) + (tile * nx + row)
        inside_x = jnp.where(rows < nx * n_tile - 1, 1.0, 0.0)

        def body(z, carry):
            inside_z = jnp.where(slab * nz + z < nz * n_slab - 1, 1.0, 0.0)
            here = extra[it, z, row : row + ROWS, :]
            ahead_z = extra[it, z + 1, row : row + ROWS, :]
            ahead_x = extra[it, z, row + 1 : row + 1 + ROWS, :]
            ahead_y = pltpu.roll(here, ny - 1, 1)
            if it == 0:
                old_z = start_p[0, z, row : row + ROWS, :]
                old_x = start_p[1, z, row : row + ROWS, :]
                old_y = start_p[2, z, row : row + ROWS, :]
                current = here
            else:
                old_z = dual_z[it - 1, z + 1, row : row + ROWS, :]
                old_x = dual_x[it - 1, z, ROWS + row : ROWS + row + ROWS, :]
                old_y = dual_y[it - 1, z, row : row + ROWS, :]
                current = value[it - 1, z, row : row + ROWS, :]
            moved_z = old_z + (0.25 * inside_z) * (ahead_z - here)
            moved_x = old_x + (0.25 * inside_x) * (ahead_x - here)
            moved_y = old_y + (0.25 * inside_y) * (ahead_y - here)
            size = moved_z * moved_z + moved_x * moved_x + moved_y * moved_y
            scale = lax.rsqrt(jnp.maximum(size, 1.0))
            new_y = moved_y * (scale * inside_y)
            dual_z[it, z + 1, row : row + ROWS, :] = moved_z * (scale * inside_z)
            dual_x[it, z, ROWS + row : ROWS + row + ROWS, :] = moved_x * (scale * inside_x)
            dual_y[it, z, row : row + ROWS, :] = new_y
            part[z, row : row + ROWS, :] = current + 0.25 * (new_y - pltpu.roll(new_y, 1, 1))
            return carry

        lax.fori_loop(low, high, body, 0)

    def over(low, high, body):
        def step(i, carry):
            z = low + lax.div(i, chunks)
            body(z, pl.ds(pl.multiple_of(lax.rem(i, chunks) * chunk, chunk), chunk))
            return carry

        lax.fori_loop(0, (high - low) * chunks, step, 0)

    def add_votes(k, z, rows, lanes, sums):
        shift = (slab * nz + z).astype(jnp.float32) * (UNIT / BAND)
        for view in range(VIEWS):
            reach = jnp.maximum(batch[k, view, rows, lanes] - shift, 0.0)
            clipped = [jnp.minimum(reach, UNIT + 0.1 * i) for i in range(BINS)]
            sums = clipped if sums is None else [s + c for s, c in zip(sums, clipped)]
        return sums

    def votes_pass(k, group, low, high):
        rows = pl.ds(ROWS * group, ROWS)

        def body(z, lanes):
            sums = add_votes(k, z, rows, lanes, [votes[i, z, rows, lanes] for i in range(BINS)])
            for i in range(BINS):
                votes[i, z, rows, lanes] = sums[i]

        over(low, high, body)

    def field_pass(it, group, low, high):
        row = ROWS * group
        rows = pl.ds(row, ROWS)

        def body(z, lanes):
            if it == 0:
                sums = add_votes(0, z, rows, lanes, None)
                for i in range(BINS):
                    votes[i, z, rows, lanes] = sums[i]
            else:
                sums = [votes[i, z, rows, lanes] for i in range(BINS)]
            moved = dual_z[it, z + 1, rows, lanes] - dual_z[it, z, rows, lanes]
            moved = moved + (
                dual_x[it, z, pl.ds(ROWS + row, ROWS), lanes]
                - dual_x[it, z, pl.ds(ROWS + row - 1, ROWS), lanes]
            )
            values = part[z, rows, lanes] + 0.25 * moved
            total = sums[0] * (0.05 / UNIT)
            base = values - total
            best = jnp.maximum(base, jnp.minimum(values + total, -1.0))
            for i in range(1, BINS):
                centre = -1.0 + 2.0 * i / (BINS - 1)
                best = jnp.maximum(
                    best, jnp.minimum(base + (sums[i] - sums[i - 1]), centre)
                )
            value[it, z, rows, lanes] = best
            if it == 0:
                extra[1, z, rows, lanes] = 2.0 * best - extra[0, z, rows, lanes]

        over(low, high, body)

    for k in range(ITERS):
        first_copy(k).start()
    into_field.wait()
    send_halo(0, 0)
    pack_extra(0)
    send_halo(0, 1)
    pass_on(0, 0)
    pass_on(1, 0)
    into_dual.wait()
    for group in range(groups - 1):
        dual_pass(0, group, 0, nz - 1)
    take_halo(0, 0)
    take_halo(0, 1)
    for stage in range(1, last - 1):
        pass_on(0, stage)
    for group in range(groups):
        dual_pass(0, group, nz - 1, nz)
    send_halo(0, 2)
    dual_pass(0, groups - 1, 0, nz - 1)
    pack_dual(0)
    send_halo(0, 3)
    for stage in range(1, last - 1):
        pass_on(1, stage)
    if last > 1:
        pass_on(0, last - 1)
    take_halo(0, 2)
    take_halo(0, 3)
    last_copy(0).wait_recv()

    for group in range(groups):
        field_pass(0, group, 0, 1)
    send_halo(1, 0)
    field_pass(0, 0, 1, nz)
    pack_extra(1)
    send_halo(1, 1)
    if last > 1:
        pass_on(1, last - 1)
    for group in range(1, groups):
        field_pass(0, group, 1, nz)
    for group in range(groups - 1):
        dual_pass(1, group, 0, nz - 1)
    last_copy(1).wait_recv()
    votes_pass(1, groups - 1, 0, nz)
    take_halo(1, 0)
    take_halo(1, 1)
    for group in range(groups):
        dual_pass(1, group, nz - 1, nz)
    send_halo(1, 2)
    dual_pass(1, groups - 1, 0, nz - 1)
    pack_dual(1)
    send_halo(1, 3)
    out_dual = [
        pltpu.make_async_copy(
            dual_z.at[1, pl.ds(1, nz)], dual_out.at[0], local_sem.at[4]
        ),
        pltpu.make_async_copy(
            dual_x.at[1, pl.ds(0, nz), pl.ds(ROWS, nx)], dual_out.at[1], local_sem.at[5]
        ),
        pltpu.make_async_copy(dual_y.at[1], dual_out.at[2], local_sem.at[6]),
    ]
    for copy in out_dual:
        copy.start()
    for group in range(groups - 1):
        votes_pass(1, group, 0, nz)
    for group in range(1, groups):
        field_pass(1, group, 1, nz)
    take_halo(1, 2)
    take_halo(1, 3)
    for group in range(groups):
        field_pass(1, group, 0, 1)
    field_pass(1, 0, 1, nz)
    out_field = pltpu.make_async_copy(value.at[1], field_out, local_sem.at[7])
    out_field.start()

    for k in range(ITERS):
        first_copy(k).wait_send()
        for stage in range(1, last):
            for piece in range(2):
                middle_copy(k, stage, piece).wait_send()
        last_copy(k).wait_send()
    for it in range(ITERS):
        for kind in range(4):
            sent_halo(it, kind)
    for copy in out_dual:
        copy.wait()
    out_field.wait()


def per_device(n_slab, n_tile, field, dual, depth, owner, visible):
    nz, nx, ny = field.shape
    stages = 1
    while 2**stages < n_slab:
        stages += 1
    slots = stages + 1
    f32 = jnp.float32
    anywhere = pl.BlockSpec(memory_space=pl.ANY)
    scalars = pl.BlockSpec(memory_space=pltpu.SMEM)
    return pl.pallas_call(
        functools.partial(kernel, n_slab, n_tile),
        out_shape=(
            jax.ShapeDtypeStruct(field.shape, f32),
            jax.ShapeDtypeStruct(dual.shape, f32),
        ),
        in_specs=[scalars, scalars, anywhere, anywhere, anywhere],
        out_specs=(anywhere, anywhere),
        scratch_shapes=[
            pltpu.VMEM((ITERS, nz + 1, nx + 8, ny), f32),
            pltpu.VMEM((3, nz, nx, ny), f32),
            pltpu.VMEM((ITERS, nz + 1, nx, ny), f32),
            pltpu.VMEM((ITERS, nz, nx + 8, ny), f32),
            pltpu.VMEM((ITERS, nz, nx, ny), f32),
            pltpu.VMEM((nz, nx, ny), f32),
            pltpu.VMEM((ITERS, nz, nx, ny), f32),
            pltpu.VMEM((BINS, nz, nx, ny), f32),
            pltpu.VMEM((ITERS, HALF, nx, ny), f32),
            pltpu.VMEM((ITERS, slots, HALF, nx, ny), f32),
            pltpu.VMEM((ITERS, slots, HALF, nx, ny), f32),
            pltpu.VMEM((ITERS, VIEWS, nx, ny), f32),
            pltpu.VMEM((ITERS, 2, nz, ny), f32),
            pltpu.VMEM((ITERS, 2, nz, ny), f32),
            pltpu.SemaphoreType.DMA((ITERS, slots, 2)),
            pltpu.SemaphoreType.DMA((ITERS, slots, 2)),
            pltpu.SemaphoreType.DMA((ITERS, 4)),
            pltpu.SemaphoreType.DMA((ITERS, 4)),
            pltpu.SemaphoreType.DMA((8,)),
        ],
        compiler_params=pltpu.CompilerParams(
            collective_id=0, has_side_effects=True, vmem_limit_bytes=40 * 2**20
        ),
        name="merge",
    )(owner, visible, field, dual, depth)


def solution(mesh):
    placed = (
        P("slab", "tile", None),
        P(None, "slab", "tile", None),
        P("slab", None, None, "tile", None),
        P(),
        P(None, None, "tile"),
    )
    return jax.shard_map(
        functools.partial(per_device, mesh.shape["slab"], mesh.shape["tile"]),
        mesh=mesh,
        in_specs=placed,
        out_specs=(P("slab", "tile", None), P(None, "slab", "tile", None)),
        check_vma=False,
    )
```

```python
import functools

import jax
import jax.numpy as jnp
from jax import lax
from jax.experimental import pallas as pl
from jax.experimental.pallas import tpu as pltpu
from jax.sharding import PartitionSpec as P

VIEWS = 4
BINS = 8
BAND = 6
ITERS = 2

ROWS = 8
UNIT = 0.35
HALF = VIEWS // 2
MESH = pl.DeviceIdType.MESH


def kernel(
    n_slab,
    n_tile,
    owner_in,
    visible_in,
    field_ref,
    dual_ref,
    depth_ref,
    field_out,
    dual_out,
    extra,
    start_p,
    dual_z,
    dual_x,
    dual_y,
    part,
    value,
    votes,
    mine,
    got,
    kept,
    batch,
    row_send,
    row_recv,
    depth_send,
    depth_recv,
    halo_send,
    halo_recv,
    local_sem,
    owner_ref,
    visible_ref,
):
    nz, nx, ny = field_ref.shape
    groups = nx // ROWS
    chunk = min(512, ny)
    chunks = ny // chunk
    slab = lax.axis_index("slab")
    tile = lax.axis_index("tile")
    bits = []
    while 2 ** len(bits) < n_slab:
        bits.append(len(bits))
    middle = bits[1:]
    order = (middle, middle[::-1])
    last = len(middle) + 1
    side = [lax.rem(lax.div(slab, 2**b), 2) for b in bits]
    partner = [slab + 2**b * (1 - 2 * side[b]) for b in bits]
    core = side[0]
    first_slab, last_slab = slab == 0, slab == n_slab - 1
    first_tile, last_tile = tile == 0, tile == n_tile - 1

    into_field = pltpu.make_async_copy(
        field_ref, extra.at[0, pl.ds(0, nz), pl.ds(0, nx)], local_sem.at[0]
    )
    into_dual = pltpu.make_async_copy(dual_ref, start_p, local_sem.at[1])
    into_mine = [
        pltpu.make_async_copy(
            depth_ref.at[0, k, pl.ds(HALF * core, HALF)], mine.at[k], local_sem.at[2 + k]
        )
        for k in range(ITERS)
    ]
    into_owner = pltpu.make_async_copy(owner_in, owner_ref, local_sem.at[8])
    into_visible = pltpu.make_async_copy(visible_in, visible_ref, local_sem.at[9])
    into_owner.start()
    into_visible.start()
    into_mine[0].start()
    into_field.start()
    into_mine[1].start()
    into_dual.start()

    barrier = pltpu.get_barrier_semaphore()
    for b in bits:
        pl.semaphore_signal(
            barrier, inc=1, device_id={"slab": partner[b]}, device_id_type=MESH
        )
    greeted = len(bits)
    for axis, place, here, there in (
        ("slab", slab, first_slab, -1),
        ("slab", slab, last_slab, 1),
        ("tile", tile, first_tile, -1),
        ("tile", tile, last_tile, 1),
    ):

        @pl.when(jnp.logical_not(here))
        def _(axis=axis, place=place, there=there):
            pl.semaphore_signal(
                barrier, inc=1, device_id={axis: place + there}, device_id_type=MESH
            )

    inner = [jnp.where(edge, 0, 1) for edge in (first_slab, last_slab, first_tile, last_tile)]
    pl.semaphore_wait(barrier, greeted + inner[0] + inner[1] + inner[2] + inner[3])

    def exchange(k, stage, piece, source, target, b):
        return pltpu.make_async_remote_copy(
            src_ref=source,
            dst_ref=target,
            send_sem=depth_send.at[k, stage, piece],
            recv_sem=depth_recv.at[k, stage, piece],
            device_id={"slab": partner[b]},
            device_id_type=MESH,
        )

    def first_copy(k):
        return exchange(
            k,
            0,
            0,
            depth_ref.at[0, k, pl.ds(HALF * (1 - core), HALF)],
            got.at[k, 0],
            0,
        )

    def middle_copy(k, stage, piece):
        return exchange(
            k,
            stage,
            piece,
            kept.at[k, stage - 1, piece],
            got.at[k, stage, piece],
            order[piece][stage - 1],
        )

    def last_copy(k):
        there = batch.at[k, pl.ds(HALF * core, HALF)]
        return exchange(k, last, 0, there, there, 0)

    def owned(k, b):
        return lax.rem(lax.div(owner_ref[k], 2**b), 2) == side[b]

    def scaled(k, piece, depth):
        seen = jnp.where(
            core == 0, visible_ref[k, 0, piece], visible_ref[k, 0, HALF + piece]
        )
        return jnp.where(seen == 1, depth * (UNIT / BAND) + 2.0 * UNIT, -1e6)

    def keep(k, stage, piece, chosen):
        if stage < last - 1:
            kept[k, stage, piece] = chosen
        else:
            batch[k, HALF * core + piece] = scaled(k, piece, chosen)

    def forward(k, stage, piece):
        if stage == 0:
            keep(k, 0, piece, jnp.where(owned(k, 0), mine[k, piece], got[k, 0, piece]))
        else:
            b = order[piece][stage - 1]
            keep(
                k,
                stage,
                piece,
                jnp.where(owned(k, b), kept[k, stage - 1, piece], got[k, stage, piece]),
            )

    def pass_on(k, stage):
        if stage == 0:
            into_mine[k].wait()
            first_copy(k).wait_recv()
        for piece in range(2):
            if stage > 0:
                middle_copy(k, stage, piece).wait_recv()
            forward(k, stage, piece)
            if stage < last - 1:
                middle_copy(k, stage + 1, piece).start()
        if stage == last - 1:
            last_copy(k).start()

    def halo(it, kind):
        if kind == 0:
            source, target = extra.at[it, 0, pl.ds(0, nx)], extra.at[it, nz, pl.ds(0, nx)]
            device = {"slab": slab - 1}
        elif kind == 1:
            source, target = row_send.at[it, 0], row_recv.at[it, 0]
            device = {"tile": tile - 1}
        elif kind == 2:
            source, target = dual_z.at[it, nz], dual_z.at[it, 0]
            device = {"slab": slab + 1}
        else:
            source, target = row_send.at[it, 1], row_recv.at[it, 1]
            device = {"tile": tile + 1}
        return pltpu.make_async_remote_copy(
            src_ref=source,
            dst_ref=target,
            send_sem=halo_send.at[it, kind],
            recv_sem=halo_recv.at[it, kind],
            device_id=device,
            device_id_type=MESH,
        )

    sends_not = (first_slab, first_tile, last_slab, last_tile)
    gets_not = (last_slab, last_tile, first_slab, first_tile)

    def send_halo(it, kind):
        @pl.when(jnp.logical_not(sends_not[kind]))
        def _():
            halo(it, kind).start()

    def sent_halo(it, kind):
        @pl.when(jnp.logical_not(sends_not[kind]))
        def _():
            halo(it, kind).wait_send()

    def take_halo(it, kind):
        @pl.when(jnp.logical_not(gets_not[kind]))
        def _():
            halo(it, kind).wait_recv()
            for z in range(nz):
                if kind == 1:
                    extra[it, z, nx : nx + 1, :] = row_recv[it, 0, z : z + 1, :]
                if kind == 3:
                    dual_x[it, z, ROWS - 1 : ROWS, :] = row_recv[it, 1, z : z + 1, :]

        @pl.when(gets_not[kind])
        def _():
            if kind == 0:
                extra[it, nz, 0:nx, :] = jnp.zeros((nx, ny), jnp.float32)
            if kind == 2:
                dual_z[it, 0] = jnp.zeros((nx, ny), jnp.float32)
            for z in range(nz):
                if kind == 1:
                    extra[it, z, nx : nx + 1, :] = jnp.zeros((1, ny), jnp.float32)
                if kind == 3:
                    dual_x[it, z, ROWS - 1 : ROWS, :] = jnp.zeros((1, ny), jnp.float32)

    def pack_extra(it):
        for z in range(nz):
            row_send[it, 0, z : z + 1, :] = extra[it, z, 0:1, :]

    def pack_dual(it):
        for z in range(nz):
            row_send[it, 1, z : z + 1, :] = dual_x[it, z, ROWS + nx - 1 : ROWS + nx, :]

    def dual_pass(it, group, low, high):
        row = ROWS * group
        lane = lax.broadcasted_iota(jnp.int32, (ROWS, ny), 1)
        inside_y = jnp.where(lane < ny - 1, 1.0, 0.0)
        rows = lax.broadcasted_iota(jnp.int32, (ROWS, ny), 0) + (tile * nx + row)
        inside_x = jnp.where(rows < nx * n_tile - 1, 1.0, 0.0)

        def body(z, carry):
            inside_z = jnp.where(slab * nz + z < nz * n_slab - 1, 1.0, 0.0)
            here = extra[it, z, row : row + ROWS, :]
            ahead_z = extra[it, z + 1, row : row + ROWS, :]
            ahead_x = extra[it, z, row + 1 : row + 1 + ROWS, :]
            ahead_y = pltpu.roll(here, ny - 1, 1)
            if it == 0:
                old_z = start_p[0, z, row : row + ROWS, :]
                old_x = start_p[1, z, row : row + ROWS, :]
                old_y = start_p[2, z, row : row + ROWS, :]
                current = here
            else:
                old_z = dual_z[it - 1, z + 1, row : row + ROWS, :]
                old_x = dual_x[it - 1, z, ROWS + row : ROWS + row + ROWS, :]
                old_y = dual_y[it - 1, z, row : row + ROWS, :]
                current = value[it - 1, z, row : row + ROWS, :]
            moved_z = old_z + (0.25 * inside_z) * (ahead_z - here)
            moved_x = old_x + (0.25 * inside_x) * (ahead_x - here)
            moved_y = old_y + (0.25 * inside_y) * (ahead_y - here)
            size = moved_z * moved_z + moved_x * moved_x + moved_y * moved_y
            scale = lax.rsqrt(jnp.maximum(size, 1.0))
            new_y = moved_y * (scale * inside_y)
            dual_z[it, z + 1, row : row + ROWS, :] = moved_z * (scale * inside_z)
            dual_x[it, z, ROWS + row : ROWS + row + ROWS, :] = moved_x * (scale * inside_x)
            dual_y[it, z, row : row + ROWS, :] = new_y
            part[z, row : row + ROWS, :] = current + 0.25 * (new_y - pltpu.roll(new_y, 1, 1))
            return carry

        lax.fori_loop(low, high, body, 0)

    def over(low, high, body):
        def step(i, carry):
            z = low + lax.div(i, chunks)
            body(z, pl.ds(pl.multiple_of(lax.rem(i, chunks) * chunk, chunk), chunk))
            return carry

        lax.fori_loop(0, (high - low) * chunks, step, 0)

    def add_votes(k, z, rows, lanes, sums):
        shift = (slab * nz + z).astype(jnp.float32) * (UNIT / BAND)
        for view in range(VIEWS):
            reach = jnp.maximum(batch[k, view, rows, lanes] - shift, 0.0)
            clipped = [jnp.minimum(reach, UNIT + 0.1 * i) for i in range(BINS)]
            sums = clipped if sums is None else [s + c for s, c in zip(sums, clipped)]
        return sums

    def field_pass(it, group, low, high):
        row = ROWS * group
        rows = pl.ds(row, ROWS)

        def body(z, lanes):
            if it == 0:
                sums = add_votes(0, z, rows, lanes, None)
                for i in range(BINS):
                    votes[i, z, rows, lanes] = sums[i]
            else:
                before = [votes[i, z, rows, lanes] for i in range(BINS)]
                sums = add_votes(1, z, rows, lanes, before)
            moved = dual_z[it, z + 1, rows, lanes] - dual_z[it, z, rows, lanes]
            moved = moved + (
                dual_x[it, z, pl.ds(ROWS + row, ROWS), lanes]
                - dual_x[it, z, pl.ds(ROWS + row - 1, ROWS), lanes]
            )
            values = part[z, rows, lanes] + 0.25 * moved
            total = sums[0] * (0.05 / UNIT)
            base = values - total
            best = jnp.maximum(base, jnp.minimum(values + total, -1.0))
            for i in range(1, BINS):
                centre = -1.0 + 2.0 * i / (BINS - 1)
                best = jnp.maximum(
                    best, jnp.minimum(base + (sums[i] - sums[i - 1]), centre)
                )
            value[it, z, rows, lanes] = best
            if it == 0:
                extra[1, z, rows, lanes] = 2.0 * best - extra[0, z, rows, lanes]

        over(low, high, body)

    first_copy(0).start()
    into_field.wait()
    pack_extra(0)
    into_owner.wait()
    into_visible.wait()
    pass_on(0, 0)
    send_halo(0, 0)
    send_halo(0, 1)
    first_copy(1).start()
    into_dual.wait()
    for group in range(groups - 1):
        dual_pass(0, group, 0, nz - 1)
    for stage in range(1, last - 1):
        pass_on(0, stage)
    take_halo(0, 0)
    take_halo(0, 1)
    for group in range(groups):
        dual_pass(0, group, nz - 1, nz)
    send_halo(0, 2)
    dual_pass(0, groups - 1, 0, nz - 1)
    pack_dual(0)
    send_halo(0, 3)
    pass_on(1, 0)
    if last > 1:
        pass_on(0, last - 1)
    take_halo(0, 2)
    take_halo(0, 3)
    last_copy(0).wait_recv()

    for group in range(groups):
        field_pass(0, group, 0, 1)
    send_halo(1, 0)
    for stage in range(1, last - 1):
        pass_on(1, stage)
    field_pass(0, 0, 1, nz)
    pack_extra(1)
    send_halo(1, 1)
    for group in range(1, groups):
        field_pass(0, group, 1, nz)
    if last > 1:
        pass_on(1, last - 1)
    for group in range(groups - 1):
        dual_pass(1, group, 0, nz - 1)
    take_halo(1, 0)
    take_halo(1, 1)
    for group in range(groups):
        dual_pass(1, group, nz - 1, nz)
    send_halo(1, 2)
    dual_pass(1, groups - 1, 0, nz - 1)
    pack_dual(1)
    send_halo(1, 3)
    out_dual = [
        pltpu.make_async_copy(
            dual_z.at[1, pl.ds(1, nz)], dual_out.at[0], local_sem.at[4]
        ),
        pltpu.make_async_copy(
            dual_x.at[1, pl.ds(0, nz), pl.ds(ROWS, nx)], dual_out.at[1], local_sem.at[5]
        ),
        pltpu.make_async_copy(dual_y.at[1], dual_out.at[2], local_sem.at[6]),
    ]
    for copy in out_dual:
        copy.start()
    last_copy(1).wait_recv()
    for group in range(1, groups):
        field_pass(1, group, 1, nz)
    take_halo(1, 2)
    take_halo(1, 3)
    for group in range(groups):
        field_pass(1, group, 0, 1)
    field_pass(1, 0, 1, nz)
    out_field = pltpu.make_async_copy(value.at[1], field_out, local_sem.at[7])
    out_field.start()

    for k in range(ITERS):
        first_copy(k).wait_send()
        for stage in range(1, last):
            for piece in range(2):
                middle_copy(k, stage, piece).wait_send()
        last_copy(k).wait_send()
    for it in range(ITERS):
        for kind in range(4):
            sent_halo(it, kind)
    for copy in out_dual:
        copy.wait()
    out_field.wait()


def per_device(n_slab, n_tile, field, dual, depth, owner, visible):
    nz, nx, ny = field.shape
    stages = 1
    while 2**stages < n_slab:
        stages += 1
    slots = stages + 1
    f32 = jnp.float32
    anywhere = pl.BlockSpec(memory_space=pl.ANY)
    return pl.pallas_call(
        functools.partial(kernel, n_slab, n_tile),
        out_shape=(
            jax.ShapeDtypeStruct(field.shape, f32),
            jax.ShapeDtypeStruct(dual.shape, f32),
        ),
        in_specs=[anywhere] * 5,
        out_specs=(anywhere, anywhere),
        scratch_shapes=[
            pltpu.VMEM((ITERS, nz + 1, nx + 8, ny), f32),
            pltpu.VMEM((3, nz, nx, ny), f32),
            pltpu.VMEM((ITERS, nz + 1, nx, ny), f32),
            pltpu.VMEM((ITERS, nz, nx + 8, ny), f32),
            pltpu.VMEM((ITERS, nz, nx, ny), f32),
            pltpu.VMEM((nz, nx, ny), f32),
            pltpu.VMEM((ITERS, nz, nx, ny), f32),
            pltpu.VMEM((BINS, nz, nx, ny), f32),
            pltpu.VMEM((ITERS, HALF, nx, ny), f32),
            pltpu.VMEM((ITERS, slots, HALF, nx, ny), f32),
            pltpu.VMEM((ITERS, slots, HALF, nx, ny), f32),
            pltpu.VMEM((ITERS, VIEWS, nx, ny), f32),
            pltpu.VMEM((ITERS, 2, nz, ny), f32),
            pltpu.VMEM((ITERS, 2, nz, ny), f32),
            pltpu.SemaphoreType.DMA((ITERS, slots, 2)),
            pltpu.SemaphoreType.DMA((ITERS, slots, 2)),
            pltpu.SemaphoreType.DMA((ITERS, 4)),
            pltpu.SemaphoreType.DMA((ITERS, 4)),
            pltpu.SemaphoreType.DMA((10,)),
            pltpu.SMEM(owner.shape, jnp.int32),
            pltpu.SMEM((ITERS, 1, VIEWS), jnp.int32),
        ],
        compiler_params=pltpu.CompilerParams(
            collective_id=0, has_side_effects=True, vmem_limit_bytes=64 * 2**20
        ),
        name="merge",
    )(owner, jnp.swapaxes(visible, 1, 2), field, dual, depth)


def solution(mesh):
    placed = (
        P("slab", "tile", None),
        P(None, "slab", "tile", None),
        P("slab", None, None, "tile", None),
        P(),
        P(None, None, "tile"),
    )
    return jax.shard_map(
        functools.partial(per_device, mesh.shape["slab"], mesh.shape["tile"]),
        mesh=mesh,
        in_specs=placed,
        out_specs=(P("slab", "tile", None), P(None, "slab", "tile", None)),
        check_vma=False,
    )
```

```python
import functools

import jax
import jax.numpy as jnp
from jax import lax
from jax.experimental import pallas as pl
from jax.experimental.pallas import tpu as pltpu
from jax.sharding import PartitionSpec as P

VIEWS = 4
BINS = 8
BAND = 6
ITERS = 2

VMEM = 64 * 2**20 - 448 * 1024
ROWS = 8
UNIT = 0.35
HALF = VIEWS // 2
MESH = pl.DeviceIdType.MESH


def kernel(
    n_slab,
    n_tile,
    owner_in,
    visible_in,
    field_ref,
    dual_ref,
    depth_ref,
    field_out,
    dual_out,
    extra,
    start_p,
    dual_z,
    dual_x,
    dual_y,
    part,
    value,
    votes,
    mine,
    got,
    kept,
    batch,
    row_send,
    row_recv,
    depth_send,
    depth_recv,
    halo_send,
    halo_recv,
    local_sem,
    owner_ref,
    visible_ref,
):
    nz, nx, ny = field_ref.shape
    groups = nx // ROWS
    chunk = min(512, ny)
    chunks = ny // chunk
    slab = lax.axis_index("slab")
    tile = lax.axis_index("tile")
    bits = []
    while 2 ** len(bits) < n_slab:
        bits.append(len(bits))
    middle = bits[1:]
    order = (middle, middle[::-1])
    last = len(middle) + 1
    side = [lax.rem(lax.div(slab, 2**b), 2) for b in bits]
    partner = [slab + 2**b * (1 - 2 * side[b]) for b in bits]
    core = side[0]
    first_slab, last_slab = slab == 0, slab == n_slab - 1
    first_tile, last_tile = tile == 0, tile == n_tile - 1

    barrier = pltpu.get_barrier_semaphore()
    for b in bits:
        pl.semaphore_signal(
            barrier, inc=1, device_id={"slab": partner[b]}, device_id_type=MESH
        )
    greeted = len(bits)
    for axis, place, here, there in (
        ("slab", slab, first_slab, -1),
        ("slab", slab, last_slab, 1),
        ("tile", tile, first_tile, -1),
        ("tile", tile, last_tile, 1),
    ):

        @pl.when(jnp.logical_not(here))
        def _(axis=axis, place=place, there=there):
            pl.semaphore_signal(
                barrier, inc=1, device_id={axis: place + there}, device_id_type=MESH
            )

    into_field = pltpu.make_async_copy(
        field_ref, extra.at[0, pl.ds(0, nz), pl.ds(0, nx)], local_sem.at[0]
    )
    into_dual = pltpu.make_async_copy(dual_ref, start_p, local_sem.at[1])
    into_mine = [
        pltpu.make_async_copy(
            depth_ref.at[0, k, pl.ds(HALF * core, HALF)], mine.at[k], local_sem.at[2 + k]
        )
        for k in range(ITERS)
    ]
    into_owner = pltpu.make_async_copy(owner_in, owner_ref, local_sem.at[8])
    into_visible = pltpu.make_async_copy(visible_in, visible_ref, local_sem.at[9])
    into_owner.start()
    into_visible.start()
    into_mine[0].start()
    into_field.start()
    into_mine[1].start()
    into_dual.start()

    inner = [jnp.where(edge, 0, 1) for edge in (first_slab, last_slab, first_tile, last_tile)]
    pl.semaphore_wait(barrier, greeted + inner[0] + inner[1] + inner[2] + inner[3])

    def exchange(k, stage, piece, source, target, b):
        return pltpu.make_async_remote_copy(
            src_ref=source,
            dst_ref=target,
            send_sem=depth_send.at[k, stage, piece],
            recv_sem=depth_recv.at[k, stage, piece],
            device_id={"slab": partner[b]},
            device_id_type=MESH,
        )

    def first_copy(k):
        return exchange(
            k,
            0,
            0,
            depth_ref.at[0, k, pl.ds(HALF * (1 - core), HALF)],
            got.at[k, 0],
            0,
        )

    def middle_copy(k, stage, piece):
        return exchange(
            k,
            stage,
            piece,
            kept.at[k, stage - 1, piece],
            got.at[k, stage, piece],
            order[piece][stage - 1],
        )

    def last_copy(k):
        there = batch.at[k, pl.ds(HALF * core, HALF)]
        return exchange(k, last, 0, there, there, 0)

    def owned(k, b):
        return lax.rem(lax.div(owner_ref[k], 2**b), 2) == side[b]

    def scaled(k, piece, depth):
        seen = jnp.where(
            core == 0, visible_ref[k, 0, piece], visible_ref[k, 0, HALF + piece]
        )
        return jnp.where(seen == 1, depth * (UNIT / BAND) + 2.0 * UNIT, -1e6)

    def keep(k, stage, piece, chosen):
        if stage < last - 1:
            kept[k, stage, piece] = chosen
        else:
            batch[k, HALF * core + piece] = scaled(k, piece, chosen)

    def forward(k, stage, piece):
        if stage == 0:
            keep(k, 0, piece, jnp.where(owned(k, 0), mine[k, piece], got[k, 0, piece]))
        else:
            b = order[piece][stage - 1]
            keep(
                k,
                stage,
                piece,
                jnp.where(owned(k, b), kept[k, stage - 1, piece], got[k, stage, piece]),
            )

    def pass_on(k, stage):
        if stage == 0:
            into_mine[k].wait()
            first_copy(k).wait_recv()
        for piece in range(2):
            if stage > 0:
                middle_copy(k, stage, piece).wait_recv()
            forward(k, stage, piece)
            if stage < last - 1:
                middle_copy(k, stage + 1, piece).start()
        if stage == last - 1:
            last_copy(k).start()

    def halo(it, kind):
        if kind == 0:
            source, target = extra.at[it, 0, pl.ds(0, nx)], extra.at[it, nz, pl.ds(0, nx)]
            device = {"slab": slab - 1}
        elif kind == 1:
            source, target = row_send.at[it, 0], row_recv.at[it, 0]
            device = {"tile": tile - 1}
        elif kind == 2:
            source, target = dual_z.at[it, nz], dual_z.at[it, 0]
            device = {"slab": slab + 1}
        else:
            source, target = row_send.at[it, 1], row_recv.at[it, 1]
            device = {"tile": tile + 1}
        return pltpu.make_async_remote_copy(
            src_ref=source,
            dst_ref=target,
            send_sem=halo_send.at[it, kind],
            recv_sem=halo_recv.at[it, kind],
            device_id=device,
            device_id_type=MESH,
        )

    sends_not = (first_slab, first_tile, last_slab, last_tile)
    gets_not = (last_slab, last_tile, first_slab, first_tile)

    def send_halo(it, kind):
        @pl.when(jnp.logical_not(sends_not[kind]))
        def _():
            halo(it, kind).start()

    def sent_halo(it, kind):
        @pl.when(jnp.logical_not(sends_not[kind]))
        def _():
            halo(it, kind).wait_send()

    def take_halo(it, kind):
        @pl.when(jnp.logical_not(gets_not[kind]))
        def _():
            halo(it, kind).wait_recv()
            for z in range(nz):
                if kind == 1:
                    extra[it, z, nx : nx + 1, :] = row_recv[it, 0, z : z + 1, :]
                if kind == 3:
                    dual_x[it, z, ROWS - 1 : ROWS, :] = row_recv[it, 1, z : z + 1, :]

        @pl.when(gets_not[kind])
        def _():
            if kind == 0:
                extra[it, nz, 0:nx, :] = jnp.zeros((nx, ny), jnp.float32)
            if kind == 2:
                dual_z[it, 0] = jnp.zeros((nx, ny), jnp.float32)
            for z in range(nz):
                if kind == 1:
                    extra[it, z, nx : nx + 1, :] = jnp.zeros((1, ny), jnp.float32)
                if kind == 3:
                    dual_x[it, z, ROWS - 1 : ROWS, :] = jnp.zeros((1, ny), jnp.float32)

    def pack_extra(it):
        for z in range(nz):
            row_send[it, 0, z : z + 1, :] = extra[it, z, 0:1, :]

    def pack_dual(it):
        for z in range(nz):
            row_send[it, 1, z : z + 1, :] = dual_x[it, z, ROWS + nx - 1 : ROWS + nx, :]

    def dual_pass(it, group, low, high):
        row = ROWS * group
        lane = lax.broadcasted_iota(jnp.int32, (ROWS, ny), 1)
        inside_y = jnp.where(lane < ny - 1, 1.0, 0.0)
        rows = lax.broadcasted_iota(jnp.int32, (ROWS, ny), 0) + (tile * nx + row)
        inside_x = jnp.where(rows < nx * n_tile - 1, 1.0, 0.0)

        def body(z, carry):
            inside_z = jnp.where(slab * nz + z < nz * n_slab - 1, 1.0, 0.0)
            here = extra[it, z, row : row + ROWS, :]
            ahead_z = extra[it, z + 1, row : row + ROWS, :]
            ahead_x = extra[it, z, row + 1 : row + 1 + ROWS, :]
            ahead_y = pltpu.roll(here, ny - 1, 1)
            if it == 0:
                old_z = start_p[0, z, row : row + ROWS, :]
                old_x = start_p[1, z, row : row + ROWS, :]
                old_y = start_p[2, z, row : row + ROWS, :]
                current = here
            else:
                old_z = dual_z[it - 1, z + 1, row : row + ROWS, :]
                old_x = dual_x[it - 1, z, ROWS + row : ROWS + row + ROWS, :]
                old_y = dual_y[it - 1, z, row : row + ROWS, :]
                current = value[it - 1, z, row : row + ROWS, :]
            moved_z = old_z + (0.25 * inside_z) * (ahead_z - here)
            moved_x = old_x + (0.25 * inside_x) * (ahead_x - here)
            moved_y = old_y + (0.25 * inside_y) * (ahead_y - here)
            size = moved_z * moved_z + moved_x * moved_x + moved_y * moved_y
            scale = lax.rsqrt(jnp.maximum(size, 1.0))
            new_y = moved_y * (scale * inside_y)
            dual_z[it, z + 1, row : row + ROWS, :] = moved_z * (scale * inside_z)
            dual_x[it, z, ROWS + row : ROWS + row + ROWS, :] = moved_x * (scale * inside_x)
            dual_y[it, z, row : row + ROWS, :] = new_y
            part[z, row : row + ROWS, :] = current + 0.25 * (new_y - pltpu.roll(new_y, 1, 1))
            return carry

        lax.fori_loop(low, high, body, 0)

    def over(low, high, body):
        def step(z, carry):
            for c in range(chunks):
                body(z, pl.ds(c * chunk, chunk))
            return carry

        lax.fori_loop(low, high, step, 0)

    def add_votes(k, z, rows, lanes, sums):
        shift = (slab * nz + z).astype(jnp.float32) * (UNIT / BAND)
        for view in range(VIEWS):
            reach = jnp.maximum(batch[k, view, rows, lanes] - shift, 0.0)
            clipped = [jnp.minimum(reach, UNIT + 0.1 * i) for i in range(BINS)]
            sums = clipped if sums is None else [s + c for s, c in zip(sums, clipped)]
        return sums

    def field_pass(it, group, low, high):
        row = ROWS * group
        rows = pl.ds(row, ROWS)

        def body(z, lanes):
            if it == 0:
                sums = add_votes(0, z, rows, lanes, None)
                for i in range(BINS):
                    votes[i, z, rows, lanes] = sums[i]
            else:
                before = [votes[i, z, rows, lanes] for i in range(BINS)]
                sums = add_votes(1, z, rows, lanes, before)
            moved = dual_z[it, z + 1, rows, lanes] - dual_z[it, z, rows, lanes]
            moved = moved + (
                dual_x[it, z, pl.ds(ROWS + row, ROWS), lanes]
                - dual_x[it, z, pl.ds(ROWS + row - 1, ROWS), lanes]
            )
            values = part[z, rows, lanes] + 0.25 * moved
            total = sums[0] * (0.05 / UNIT)
            base = values - total
            best = jnp.maximum(base, jnp.minimum(values + total, -1.0))
            for i in range(1, BINS):
                centre = -1.0 + 2.0 * i / (BINS - 1)
                best = jnp.maximum(
                    best, jnp.minimum(base + (sums[i] - sums[i - 1]), centre)
                )
            if it == ITERS - 1:
                field_out[z, rows, lanes] = best
            else:
                value[it, z, rows, lanes] = best
                extra[1, z, rows, lanes] = 2.0 * best - extra[0, z, rows, lanes]

        over(low, high, body)

    first_copy(0).start()
    into_field.wait()
    pack_extra(0)
    into_owner.wait()
    into_visible.wait()
    pass_on(0, 0)
    send_halo(0, 0)
    send_halo(0, 1)
    first_copy(1).start()
    into_dual.wait()
    for group in range(groups - 1):
        dual_pass(0, group, 0, nz - 1)
    for stage in range(1, last - 1):
        pass_on(0, stage)
    take_halo(0, 0)
    take_halo(0, 1)
    for group in range(groups):
        dual_pass(0, group, nz - 1, nz)
    send_halo(0, 2)
    dual_pass(0, groups - 1, 0, nz - 1)
    pack_dual(0)
    send_halo(0, 3)
    pass_on(1, 0)
    if last > 1:
        pass_on(0, last - 1)
    take_halo(0, 2)
    take_halo(0, 3)
    last_copy(0).wait_recv()

    for group in range(groups):
        field_pass(0, group, 0, 1)
    send_halo(1, 0)
    for stage in range(1, last - 1):
        pass_on(1, stage)
    field_pass(0, 0, 1, nz)
    pack_extra(1)
    send_halo(1, 1)
    for group in range(1, groups):
        field_pass(0, group, 1, nz)
    if last > 1:
        pass_on(1, last - 1)
    for group in range(groups - 1):
        dual_pass(1, group, 0, nz - 1)
    take_halo(1, 0)
    take_halo(1, 1)
    for group in range(groups):
        dual_pass(1, group, nz - 1, nz)
    send_halo(1, 2)
    dual_pass(1, groups - 1, 0, nz - 1)
    pack_dual(1)
    send_halo(1, 3)
    out_dual = [
        pltpu.make_async_copy(
            dual_z.at[1, pl.ds(1, nz)], dual_out.at[0], local_sem.at[4]
        ),
        pltpu.make_async_copy(
            dual_x.at[1, pl.ds(0, nz), pl.ds(ROWS, nx)], dual_out.at[1], local_sem.at[5]
        ),
        pltpu.make_async_copy(dual_y.at[1], dual_out.at[2], local_sem.at[6]),
    ]
    for copy in out_dual:
        copy.start()
    last_copy(1).wait_recv()
    for group in range(1, groups):
        field_pass(1, group, 1, nz)
    take_halo(1, 2)
    take_halo(1, 3)
    for group in range(groups):
        field_pass(1, group, 0, 1)
    field_pass(1, 0, 1, nz)

    for k in range(ITERS):
        first_copy(k).wait_send()
        for stage in range(1, last):
            for piece in range(2):
                middle_copy(k, stage, piece).wait_send()
        last_copy(k).wait_send()
    for it in range(ITERS):
        for kind in range(4):
            sent_halo(it, kind)
    for copy in out_dual:
        copy.wait()


def write_out(field_kept, dual_kept, field_out, dual_out, sem):
    copies = [pltpu.make_async_copy(field_kept, field_out, sem.at[3])]
    for c in range(3):
        copies.append(pltpu.make_async_copy(dual_kept.at[c], dual_out.at[c], sem.at[c]))
    for copy in copies:
        copy.start()
    for copy in copies:
        copy.wait()


def per_device(n_slab, n_tile, field, dual, depth, owner, visible):
    nz, nx, ny = field.shape
    stages = 1
    while 2**stages < n_slab:
        stages += 1
    slots = stages + 1
    f32 = jnp.float32
    anywhere = pl.BlockSpec(memory_space=pl.ANY)
    field_kept, dual_kept = pl.pallas_call(
        functools.partial(kernel, n_slab, n_tile),
        out_shape=(
            pltpu.VMEM(field.shape, f32),
            pltpu.VMEM(dual.shape, f32),
        ),
        in_specs=[anywhere] * 5,
        out_specs=(pl.BlockSpec(memory_space=pltpu.VMEM),) * 2,
        scratch_shapes=[
            pltpu.VMEM((ITERS, nz + 1, nx + 8, ny), f32),
            pltpu.VMEM((3, nz, nx, ny), f32),
            pltpu.VMEM((ITERS, nz + 1, nx, ny), f32),
            pltpu.VMEM((ITERS, nz, nx + 8, ny), f32),
            pltpu.VMEM((ITERS, nz, nx, ny), f32),
            pltpu.VMEM((nz, nx, ny), f32),
            pltpu.VMEM((ITERS, nz, nx, ny), f32),
            pltpu.VMEM((BINS, nz, nx, ny), f32),
            pltpu.VMEM((ITERS, HALF, nx, ny), f32),
            pltpu.VMEM((ITERS, slots, HALF, nx, ny), f32),
            pltpu.VMEM((ITERS, slots, HALF, nx, ny), f32),
            pltpu.VMEM((ITERS, VIEWS, nx, ny), f32),
            pltpu.VMEM((ITERS, 2, nz, ny), f32),
            pltpu.VMEM((ITERS, 2, nz, ny), f32),
            pltpu.SemaphoreType.DMA((ITERS, slots, 2)),
            pltpu.SemaphoreType.DMA((ITERS, slots, 2)),
            pltpu.SemaphoreType.DMA((ITERS, 4)),
            pltpu.SemaphoreType.DMA((ITERS, 4)),
            pltpu.SemaphoreType.DMA((10,)),
            pltpu.SMEM(owner.shape, jnp.int32),
            pltpu.SMEM((ITERS, 1, VIEWS), jnp.int32),
        ],
        compiler_params=pltpu.CompilerParams(
            collective_id=0, has_side_effects=True, vmem_limit_bytes=VMEM - 4 * (field.size + dual.size)
        ),
        name="merge",
    )(owner, jnp.swapaxes(visible, 1, 2), field, dual, depth)
    return pl.pallas_call(
        write_out,
        out_shape=(
            jax.ShapeDtypeStruct(field.shape, f32),
            jax.ShapeDtypeStruct(dual.shape, f32),
        ),
        in_specs=[pl.BlockSpec(memory_space=pltpu.VMEM)] * 2,
        out_specs=(anywhere, anywhere),
        scratch_shapes=[pltpu.SemaphoreType.DMA((4,))],
        name="write",
    )(field_kept, dual_kept)


def solution(mesh):
    placed = (
        P("slab", "tile", None),
        P(None, "slab", "tile", None),
        P("slab", None, None, "tile", None),
        P(),
        P(None, None, "tile"),
    )
    return jax.shard_map(
        functools.partial(per_device, mesh.shape["slab"], mesh.shape["tile"]),
        mesh=mesh,
        in_specs=placed,
        out_specs=(P("slab", "tile", None), P(None, "slab", "tile", None)),
        check_vma=False,
    )
```

```python
import functools

import jax
import jax.numpy as jnp
from jax import lax
from jax.experimental import pallas as pl
from jax.experimental.pallas import tpu as pltpu
from jax.sharding import PartitionSpec as P

VIEWS = 4
BINS = 8
BAND = 6
ITERS = 2

VMEM = 64 * 2**20 - 448 * 1024
ROWS = 8
UNIT = 0.35
HALF = VIEWS // 2
MESH = pl.DeviceIdType.MESH


def kernel(
    n_slab,
    n_tile,
    owner_in,
    visible_in,
    field_ref,
    dual_ref,
    depth_ref,
    field_out,
    dual_out,
    extra,
    start_p,
    dual_z,
    dual_x,
    dual_y,
    part,
    value,
    votes,
    mine,
    got,
    kept,
    batch,
    row_send,
    row_recv,
    depth_send,
    depth_recv,
    halo_send,
    halo_recv,
    local_sem,
    owner_ref,
    visible_ref,
):
    nz, nx, ny = field_ref.shape
    groups = nx // ROWS
    chunk = min(512, ny)
    chunks = ny // chunk
    slab = lax.axis_index("slab")
    tile = lax.axis_index("tile")
    bits = []
    while 2 ** len(bits) < n_slab:
        bits.append(len(bits))
    middle = bits[1:]
    order = (middle, middle[::-1])
    last = len(middle) + 1
    side = [lax.rem(lax.div(slab, 2**b), 2) for b in bits]
    partner = [slab + 2**b * (1 - 2 * side[b]) for b in bits]
    core = side[0]
    first_slab, last_slab = slab == 0, slab == n_slab - 1
    first_tile, last_tile = tile == 0, tile == n_tile - 1

    barrier = pltpu.get_barrier_semaphore()
    for b in bits:
        pl.semaphore_signal(
            barrier, inc=1, device_id={"slab": partner[b]}, device_id_type=MESH
        )
    greeted = len(bits)
    for axis, place, here, there in (
        ("slab", slab, first_slab, -1),
        ("slab", slab, last_slab, 1),
        ("tile", tile, first_tile, -1),
        ("tile", tile, last_tile, 1),
    ):

        @pl.when(jnp.logical_not(here))
        def _(axis=axis, place=place, there=there):
            pl.semaphore_signal(
                barrier, inc=1, device_id={axis: place + there}, device_id_type=MESH
            )

    into_field = pltpu.make_async_copy(
        field_ref, extra.at[0, pl.ds(0, nz), pl.ds(0, nx)], local_sem.at[0]
    )
    into_dual = pltpu.make_async_copy(dual_ref, start_p, local_sem.at[1])
    into_mine = [
        pltpu.make_async_copy(
            depth_ref.at[0, k, pl.ds(HALF * core, HALF)], mine.at[k], local_sem.at[2 + k]
        )
        for k in range(ITERS)
    ]
    into_owner = pltpu.make_async_copy(owner_in, owner_ref, local_sem.at[8])
    into_visible = pltpu.make_async_copy(visible_in, visible_ref, local_sem.at[9])
    into_owner.start()
    into_visible.start()
    into_mine[0].start()
    into_field.start()
    into_mine[1].start()
    into_dual.start()

    inner = [jnp.where(edge, 0, 1) for edge in (first_slab, last_slab, first_tile, last_tile)]
    pl.semaphore_wait(barrier, greeted + inner[0] + inner[1] + inner[2] + inner[3])

    def exchange(k, stage, piece, source, target, b):
        return pltpu.make_async_remote_copy(
            src_ref=source,
            dst_ref=target,
            send_sem=depth_send.at[k, stage, piece],
            recv_sem=depth_recv.at[k, stage, piece],
            device_id={"slab": partner[b]},
            device_id_type=MESH,
        )

    def first_copy(k):
        return exchange(
            k,
            0,
            0,
            depth_ref.at[0, k, pl.ds(HALF * (1 - core), HALF)],
            got.at[k, 0],
            0,
        )

    def middle_copy(k, stage, piece):
        return exchange(
            k,
            stage,
            piece,
            kept.at[k, stage - 1, piece],
            got.at[k, stage, piece],
            order[piece][stage - 1],
        )

    def last_copy(k):
        there = batch.at[k, pl.ds(HALF * core, HALF)]
        return exchange(k, last, 0, there, there, 0)

    def owned(k, b):
        return lax.rem(lax.div(owner_ref[k], 2**b), 2) == side[b]

    def scaled(k, piece, depth):
        seen = jnp.where(
            core == 0, visible_ref[k, 0, piece], visible_ref[k, 0, HALF + piece]
        )
        return jnp.where(seen == 1, depth * (UNIT / BAND) + 2.0 * UNIT, -1e6)

    def keep(k, stage, piece, chosen):
        if stage < last - 1:
            kept[k, stage, piece] = chosen
        else:
            batch[k, HALF * core + piece] = scaled(k, piece, chosen)

    def forward(k, stage, piece):
        if stage == 0:
            keep(k, 0, piece, jnp.where(owned(k, 0), mine[k, piece], got[k, 0, piece]))
        else:
            b = order[piece][stage - 1]
            keep(
                k,
                stage,
                piece,
                jnp.where(owned(k, b), kept[k, stage - 1, piece], got[k, stage, piece]),
            )

    def pass_on(k, stage):
        if stage == 0:
            into_mine[k].wait()
            first_copy(k).wait_recv()
        for piece in range(2):
            if stage > 0:
                middle_copy(k, stage, piece).wait_recv()
            forward(k, stage, piece)
            if stage < last - 1:
                middle_copy(k, stage + 1, piece).start()
        if stage == last - 1:
            last_copy(k).start()

    def halo(it, kind):
        if kind == 0:
            source, target = extra.at[it, 0, pl.ds(0, nx)], extra.at[it, nz, pl.ds(0, nx)]
            device = {"slab": slab - 1}
        elif kind == 1:
            source, target = row_send.at[it, 0], row_recv.at[it, 0]
            device = {"tile": tile - 1}
        elif kind == 2:
            source, target = dual_z.at[it, nz], dual_z.at[it, 0]
            device = {"slab": slab + 1}
        else:
            source, target = row_send.at[it, 1], row_recv.at[it, 1]
            device = {"tile": tile + 1}
        return pltpu.make_async_remote_copy(
            src_ref=source,
            dst_ref=target,
            send_sem=halo_send.at[it, kind],
            recv_sem=halo_recv.at[it, kind],
            device_id=device,
            device_id_type=MESH,
        )

    sends_not = (first_slab, first_tile, last_slab, last_tile)
    gets_not = (last_slab, last_tile, first_slab, first_tile)

    def send_halo(it, kind):
        @pl.when(jnp.logical_not(sends_not[kind]))
        def _():
            halo(it, kind).start()

    def sent_halo(it, kind):
        @pl.when(jnp.logical_not(sends_not[kind]))
        def _():
            halo(it, kind).wait_send()

    def take_halo(it, kind):
        @pl.when(jnp.logical_not(gets_not[kind]))
        def _():
            halo(it, kind).wait_recv()
            for z in range(nz):
                if kind == 1:
                    extra[it, z, nx : nx + 1, :] = row_recv[it, 0, z : z + 1, :]
                if kind == 3:
                    dual_x[it, z, ROWS - 1 : ROWS, :] = row_recv[it, 1, z : z + 1, :]

        @pl.when(gets_not[kind])
        def _():
            if kind == 0:
                extra[it, nz, 0:nx, :] = jnp.zeros((nx, ny), jnp.float32)
            if kind == 2:
                dual_z[it, 0] = jnp.zeros((nx, ny), jnp.float32)
            for z in range(nz):
                if kind == 1:
                    extra[it, z, nx : nx + 1, :] = jnp.zeros((1, ny), jnp.float32)
                if kind == 3:
                    dual_x[it, z, ROWS - 1 : ROWS, :] = jnp.zeros((1, ny), jnp.float32)

    def pack_extra(it):
        for z in range(nz):
            row_send[it, 0, z : z + 1, :] = extra[it, z, 0:1, :]

    def pack_dual(it):
        for z in range(nz):
            row_send[it, 1, z : z + 1, :] = dual_x[it, z, ROWS + nx - 1 : ROWS + nx, :]

    def dual_pass(it, group, low, high):
        row = ROWS * group
        lane = lax.broadcasted_iota(jnp.int32, (ROWS, ny), 1)
        inside_y = jnp.where(lane < ny - 1, 1.0, 0.0)
        rows = lax.broadcasted_iota(jnp.int32, (ROWS, ny), 0) + (tile * nx + row)
        inside_x = jnp.where(rows < nx * n_tile - 1, 1.0, 0.0)

        def body(z, carry):
            inside_z = jnp.where(slab * nz + z < nz * n_slab - 1, 1.0, 0.0)
            here = extra[it, z, row : row + ROWS, :]
            ahead_z = extra[it, z + 1, row : row + ROWS, :]
            ahead_x = extra[it, z, row + 1 : row + 1 + ROWS, :]
            ahead_y = pltpu.roll(here, ny - 1, 1)
            if it == 0:
                old_z = start_p[0, z, row : row + ROWS, :]
                old_x = start_p[1, z, row : row + ROWS, :]
                old_y = start_p[2, z, row : row + ROWS, :]
                current = here
            else:
                old_z = dual_z[it - 1, z + 1, row : row + ROWS, :]
                old_x = dual_x[it - 1, z, ROWS + row : ROWS + row + ROWS, :]
                old_y = dual_y[it - 1, z, row : row + ROWS, :]
                current = value[it - 1, z, row : row + ROWS, :]
            moved_z = old_z + (0.25 * inside_z) * (ahead_z - here)
            moved_x = old_x + (0.25 * inside_x) * (ahead_x - here)
            moved_y = old_y + (0.25 * inside_y) * (ahead_y - here)
            size = moved_z * moved_z + moved_x * moved_x + moved_y * moved_y
            scale = lax.rsqrt(jnp.maximum(size, 1.0))
            new_y = moved_y * (scale * inside_y)
            dual_z[it, z + 1, row : row + ROWS, :] = moved_z * (scale * inside_z)
            dual_x[it, z, ROWS + row : ROWS + row + ROWS, :] = moved_x * (scale * inside_x)
            dual_y[it, z, row : row + ROWS, :] = new_y
            part[z, row : row + ROWS, :] = current + 0.25 * (new_y - pltpu.roll(new_y, 1, 1))
            return carry

        lax.fori_loop(low, high, body, 0)

    def over(low, high, body):
        def step(z, carry):
            for c in range(chunks):
                body(z, pl.ds(c * chunk, chunk))
            return carry

        lax.fori_loop(low, high, step, 0)

    def add_votes(k, z, rows, lanes, sums):
        shift = (slab * nz + z).astype(jnp.float32) * (UNIT / BAND)
        for view in range(VIEWS):
            reach = jnp.maximum(batch[k, view, rows, lanes] - shift, 0.0)
            clipped = [jnp.minimum(reach, UNIT + 0.1 * i) for i in range(BINS)]
            sums = clipped if sums is None else [s + c for s, c in zip(sums, clipped)]
        return sums

    def field_pass(it, group, low, high):
        row = ROWS * group
        rows = pl.ds(row, ROWS)

        def body(z, lanes):
            if it == 0:
                sums = add_votes(0, z, rows, lanes, None)
                for i in range(BINS):
                    votes[i, z, rows, lanes] = sums[i]
            else:
                before = [votes[i, z, rows, lanes] for i in range(BINS)]
                sums = add_votes(1, z, rows, lanes, before)
            moved = dual_z[it, z + 1, rows, lanes] - dual_z[it, z, rows, lanes]
            moved = moved + (
                dual_x[it, z, pl.ds(ROWS + row, ROWS), lanes]
                - dual_x[it, z, pl.ds(ROWS + row - 1, ROWS), lanes]
            )
            values = part[z, rows, lanes] + 0.25 * moved
            total = sums[0] * (0.05 / UNIT)
            base = values - total
            best = jnp.maximum(base, jnp.minimum(values + total, -1.0))
            for i in range(1, BINS):
                centre = -1.0 + 2.0 * i / (BINS - 1)
                best = jnp.maximum(
                    best, jnp.minimum(base + (sums[i] - sums[i - 1]), centre)
                )
            if it == ITERS - 1:
                field_out[z, rows, lanes] = best
            else:
                value[it, z, rows, lanes] = best
                extra[1, z, rows, lanes] = 2.0 * best - extra[0, z, rows, lanes]

        over(low, high, body)

    first_copy(0).start()
    into_field.wait()
    pack_extra(0)
    into_owner.wait()
    into_visible.wait()
    pass_on(0, 0)
    send_halo(0, 0)
    send_halo(0, 1)
    first_copy(1).start()
    into_dual.wait()
    for group in range(groups - 1):
        dual_pass(0, group, 0, nz - 1)
    for stage in range(1, last - 1):
        pass_on(0, stage)
    take_halo(0, 0)
    take_halo(0, 1)
    for group in range(groups):
        dual_pass(0, group, nz - 1, nz)
    send_halo(0, 2)
    dual_pass(0, groups - 1, 0, nz - 1)
    pack_dual(0)
    send_halo(0, 3)
    pass_on(1, 0)
    if last > 1:
        pass_on(0, last - 1)
    take_halo(0, 2)
    take_halo(0, 3)
    last_copy(0).wait_recv()

    for group in range(groups):
        field_pass(0, group, 0, 1)
    send_halo(1, 0)
    for stage in range(1, last - 1):
        pass_on(1, stage)
    field_pass(0, 0, 1, nz)
    pack_extra(1)
    send_halo(1, 1)
    for group in range(1, groups):
        field_pass(0, group, 1, nz)
    if last > 1:
        pass_on(1, last - 1)
    for group in range(groups - 1):
        dual_pass(1, group, 0, nz - 1)
    take_halo(1, 0)
    take_halo(1, 1)
    for group in range(groups):
        dual_pass(1, group, nz - 1, nz)
    send_halo(1, 2)
    dual_pass(1, groups - 1, 0, nz - 1)
    pack_dual(1)
    send_halo(1, 3)
    out_dual = [
        pltpu.make_async_copy(
            dual_z.at[1, pl.ds(1, nz)], dual_out.at[0], local_sem.at[4]
        ),
        pltpu.make_async_copy(
            dual_x.at[1, pl.ds(0, nz), pl.ds(ROWS, nx)], dual_out.at[1], local_sem.at[5]
        ),
        pltpu.make_async_copy(dual_y.at[1], dual_out.at[2], local_sem.at[6]),
    ]
    for copy in out_dual:
        copy.start()
    last_copy(1).wait_recv()
    for group in range(1, groups):
        field_pass(1, group, 1, nz)
    take_halo(1, 2)
    take_halo(1, 3)
    for group in range(groups):
        field_pass(1, group, 0, 1)
    field_pass(1, 0, 1, nz)

    for k in range(ITERS):
        first_copy(k).wait_send()
        for stage in range(1, last):
            for piece in range(2):
                middle_copy(k, stage, piece).wait_send()
        last_copy(k).wait_send()
    for it in range(ITERS):
        for kind in range(4):
            sent_halo(it, kind)
    for copy in out_dual:
        copy.wait()


def write_out(field_kept, dual_kept, field_out, dual_out, sem):
    copies = [pltpu.make_async_copy(field_kept, field_out, sem.at[3])]
    for c in range(3):
        copies.append(pltpu.make_async_copy(dual_kept.at[c], dual_out.at[c], sem.at[c]))
    for copy in copies:
        copy.start()
    for copy in copies:
        copy.wait()


def per_device(n_slab, n_tile, field, dual, depth, owner, visible):
    nz, nx, ny = field.shape
    stages = 1
    while 2**stages < n_slab:
        stages += 1
    slots = stages + 1
    f32 = jnp.float32
    anywhere = pl.BlockSpec(memory_space=pl.ANY)
    field_kept, dual_kept = pl.pallas_call(
        functools.partial(kernel, n_slab, n_tile),
        out_shape=(
            pltpu.VMEM(field.shape, f32),
            pltpu.VMEM(dual.shape, f32),
        ),
        in_specs=[anywhere] * 5,
        out_specs=(pl.BlockSpec(memory_space=pltpu.VMEM),) * 2,
        scratch_shapes=[
            pltpu.VMEM((ITERS, nz + 1, nx + 8, ny), f32),
            pltpu.VMEM((3, nz, nx, ny), f32),
            pltpu.VMEM((ITERS, nz + 1, nx, ny), f32),
            pltpu.VMEM((ITERS, nz, nx + 8, ny), f32),
            pltpu.VMEM((ITERS, nz, nx, ny), f32),
            pltpu.VMEM((nz, nx, ny), f32),
            pltpu.VMEM((ITERS, nz, nx, ny), f32),
            pltpu.VMEM((BINS, nz, nx, ny), f32),
            pltpu.VMEM((ITERS, HALF, nx, ny), f32),
            pltpu.VMEM((ITERS, slots, HALF, nx, ny), f32),
            pltpu.VMEM((ITERS, slots, HALF, nx, ny), f32),
            pltpu.VMEM((ITERS, VIEWS, nx, ny), f32),
            pltpu.VMEM((ITERS, 2, nz, ny), f32),
            pltpu.VMEM((ITERS, 2, nz, ny), f32),
            pltpu.SemaphoreType.DMA((ITERS, slots, 2)),
            pltpu.SemaphoreType.DMA((ITERS, slots, 2)),
            pltpu.SemaphoreType.DMA((ITERS, 4)),
            pltpu.SemaphoreType.DMA((ITERS, 4)),
            pltpu.SemaphoreType.DMA((10,)),
            pltpu.SMEM(owner.shape, jnp.int32),
            pltpu.SMEM((ITERS, 1, VIEWS), jnp.int32),
        ],
        compiler_params=pltpu.CompilerParams(
            collective_id=0, has_side_effects=True, vmem_limit_bytes=VMEM - 4 * (field.size + dual.size)
        ),
        name="merge",
    )(owner, jnp.swapaxes(visible, 1, 2), field, dual, depth)
    return pl.pallas_call(
        write_out,
        out_shape=(
            jax.ShapeDtypeStruct(field.shape, f32),
            jax.ShapeDtypeStruct(dual.shape, f32),
        ),
        in_specs=[pl.BlockSpec(memory_space=pltpu.VMEM)] * 2,
        out_specs=(anywhere, anywhere),
        scratch_shapes=[pltpu.SemaphoreType.DMA((4,))],
        compiler_params=pltpu.CompilerParams(vmem_limit_bytes=4 * 2**20),
        name="write",
    )(field_kept, dual_kept)


def solution(mesh):
    placed = (
        P("slab", "tile", None),
        P(None, "slab", "tile", None),
        P("slab", None, None, "tile", None),
        P(),
        P(None, None, "tile"),
    )
    return jax.shard_map(
        functools.partial(per_device, mesh.shape["slab"], mesh.shape["tile"]),
        mesh=mesh,
        in_specs=placed,
        out_specs=(P("slab", "tile", None), P(None, "slab", "tile", None)),
        check_vma=False,
    )
```

```python
import functools

import jax
import jax.numpy as jnp
from jax import lax
from jax.experimental import pallas as pl
from jax.experimental.pallas import tpu as pltpu
from jax.sharding import PartitionSpec as P

VIEWS = 4
BINS = 8
BAND = 6
ITERS = 2

VMEM = 64 * 2**20 - 448 * 1024
ROWS = 8
UNIT = 0.35
HALF = VIEWS // 2
MESH = pl.DeviceIdType.MESH


def kernel(
    n_slab,
    n_tile,
    owner_in,
    visible_in,
    field_ref,
    dual_ref,
    depth_ref,
    field_out,
    dual_out,
    extra,
    start_p,
    dual_z,
    dual_x,
    dual_y,
    part,
    value,
    votes,
    mine,
    got,
    kept,
    batch,
    row_send,
    row_recv,
    depth_send,
    depth_recv,
    halo_send,
    halo_recv,
    local_sem,
    owner_ref,
    visible_ref,
):
    nz, nx, ny = field_ref.shape
    groups = nx // ROWS
    chunk = min(256, ny)
    chunks = ny // chunk
    slab = lax.axis_index("slab")
    tile = lax.axis_index("tile")
    bits = []
    while 2 ** len(bits) < n_slab:
        bits.append(len(bits))
    middle = bits[1:]
    order = (middle, middle[::-1])
    last = len(middle) + 1
    side = [lax.rem(lax.div(slab, 2**b), 2) for b in bits]
    partner = [slab + 2**b * (1 - 2 * side[b]) for b in bits]
    core = side[0]
    first_slab, last_slab = slab == 0, slab == n_slab - 1
    first_tile, last_tile = tile == 0, tile == n_tile - 1

    barrier = pltpu.get_barrier_semaphore()
    for b in bits:
        pl.semaphore_signal(
            barrier, inc=1, device_id={"slab": partner[b]}, device_id_type=MESH
        )
    greeted = len(bits)
    for axis, place, here, there in (
        ("slab", slab, first_slab, -1),
        ("slab", slab, last_slab, 1),
        ("tile", tile, first_tile, -1),
        ("tile", tile, last_tile, 1),
    ):

        @pl.when(jnp.logical_not(here))
        def _(axis=axis, place=place, there=there):
            pl.semaphore_signal(
                barrier, inc=1, device_id={axis: place + there}, device_id_type=MESH
            )

    into_field = pltpu.make_async_copy(
        field_ref, extra.at[0, pl.ds(0, nz), pl.ds(0, nx)], local_sem.at[0]
    )
    into_dual = pltpu.make_async_copy(dual_ref, start_p, local_sem.at[1])
    into_mine = [
        pltpu.make_async_copy(
            depth_ref.at[0, k, pl.ds(HALF * core, HALF)], mine.at[k], local_sem.at[2 + k]
        )
        for k in range(ITERS)
    ]
    into_owner = pltpu.make_async_copy(owner_in, owner_ref, local_sem.at[8])
    into_visible = pltpu.make_async_copy(visible_in, visible_ref, local_sem.at[9])
    into_owner.start()
    into_visible.start()
    into_mine[0].start()
    into_field.start()
    into_mine[1].start()
    into_dual.start()

    inner = [jnp.where(edge, 0, 1) for edge in (first_slab, last_slab, first_tile, last_tile)]
    pl.semaphore_wait(barrier, greeted + inner[0] + inner[1] + inner[2] + inner[3])

    def exchange(k, stage, piece, source, target, b):
        return pltpu.make_async_remote_copy(
            src_ref=source,
            dst_ref=target,
            send_sem=depth_send.at[k, stage, piece],
            recv_sem=depth_recv.at[k, stage, piece],
            device_id={"slab": partner[b]},
            device_id_type=MESH,
        )

    def first_copy(k):
        return exchange(
            k,
            0,
            0,
            depth_ref.at[0, k, pl.ds(HALF * (1 - core), HALF)],
            got.at[k, 0],
            0,
        )

    def middle_copy(k, stage, piece):
        return exchange(
            k,
            stage,
            piece,
            kept.at[k, stage - 1, piece],
            got.at[k, stage, piece],
            order[piece][stage - 1],
        )

    def last_copy(k):
        there = batch.at[k, pl.ds(HALF * core, HALF)]
        return exchange(k, last, 0, there, there, 0)

    def owned(k, b):
        return lax.rem(lax.div(owner_ref[k], 2**b), 2) == side[b]

    def scaled(k, piece, depth):
        seen = jnp.where(
            core == 0, visible_ref[k, 0, piece], visible_ref[k, 0, HALF + piece]
        )
        return jnp.where(seen == 1, depth * (UNIT / BAND) + 2.0 * UNIT, -1e6)

    def keep(k, stage, piece, chosen):
        if stage < last - 1:
            kept[k, stage, piece] = chosen
        else:
            batch[k, HALF * core + piece] = scaled(k, piece, chosen)

    def forward(k, stage, piece):
        if stage == 0:
            keep(k, 0, piece, jnp.where(owned(k, 0), mine[k, piece], got[k, 0, piece]))
        else:
            b = order[piece][stage - 1]
            keep(
                k,
                stage,
                piece,
                jnp.where(owned(k, b), kept[k, stage - 1, piece], got[k, stage, piece]),
            )

    def pass_on(k, stage):
        if stage == 0:
            into_mine[k].wait()
            first_copy(k).wait_recv()
        for piece in range(2):
            if stage > 0:
                middle_copy(k, stage, piece).wait_recv()
            forward(k, stage, piece)
            if stage < last - 1:
                middle_copy(k, stage + 1, piece).start()
        if stage == last - 1:
            last_copy(k).start()

    def halo(it, kind):
        if kind == 0:
            source, target = extra.at[it, 0, pl.ds(0, nx)], extra.at[it, nz, pl.ds(0, nx)]
            device = {"slab": slab - 1}
        elif kind == 1:
            source, target = row_send.at[it, 0], row_recv.at[it, 0]
            device = {"tile": tile - 1}
        elif kind == 2:
            source, target = dual_z.at[it, nz], dual_z.at[it, 0]
            device = {"slab": slab + 1}
        else:
            source, target = row_send.at[it, 1], row_recv.at[it, 1]
            device = {"tile": tile + 1}
        return pltpu.make_async_remote_copy(
            src_ref=source,
            dst_ref=target,
            send_sem=halo_send.at[it, kind],
            recv_sem=halo_recv.at[it, kind],
            device_id=device,
            device_id_type=MESH,
        )

    sends_not = (first_slab, first_tile, last_slab, last_tile)
    gets_not = (last_slab, last_tile, first_slab, first_tile)

    def send_halo(it, kind):
        @pl.when(jnp.logical_not(sends_not[kind]))
        def _():
            halo(it, kind).start()

    def sent_halo(it, kind):
        @pl.when(jnp.logical_not(sends_not[kind]))
        def _():
            halo(it, kind).wait_send()

    def take_halo(it, kind):
        @pl.when(jnp.logical_not(gets_not[kind]))
        def _():
            halo(it, kind).wait_recv()
            for z in range(nz):
                if kind == 1:
                    extra[it, z, nx : nx + 1, :] = row_recv[it, 0, z : z + 1, :]
                if kind == 3:
                    dual_x[it, z, ROWS - 1 : ROWS, :] = row_recv[it, 1, z : z + 1, :]

        @pl.when(gets_not[kind])
        def _():
            if kind == 0:
                extra[it, nz, 0:nx, :] = jnp.zeros((nx, ny), jnp.float32)
            if kind == 2:
                dual_z[it, 0] = jnp.zeros((nx, ny), jnp.float32)
            for z in range(nz):
                if kind == 1:
                    extra[it, z, nx : nx + 1, :] = jnp.zeros((1, ny), jnp.float32)
                if kind == 3:
                    dual_x[it, z, ROWS - 1 : ROWS, :] = jnp.zeros((1, ny), jnp.float32)

    def pack_extra(it):
        for z in range(nz):
            row_send[it, 0, z : z + 1, :] = extra[it, z, 0:1, :]

    def pack_dual(it):
        for z in range(nz):
            row_send[it, 1, z : z + 1, :] = dual_x[it, z, ROWS + nx - 1 : ROWS + nx, :]

    def dual_pass(it, group, low, high):
        row = ROWS * group
        lane = lax.broadcasted_iota(jnp.int32, (ROWS, ny), 1)
        inside_y = jnp.where(lane < ny - 1, 1.0, 0.0)
        rows = lax.broadcasted_iota(jnp.int32, (ROWS, ny), 0) + (tile * nx + row)
        inside_x = jnp.where(rows < nx * n_tile - 1, 1.0, 0.0)

        def body(z, carry):
            inside_z = jnp.where(slab * nz + z < nz * n_slab - 1, 1.0, 0.0)
            here = extra[it, z, row : row + ROWS, :]
            ahead_z = extra[it, z + 1, row : row + ROWS, :]
            ahead_x = extra[it, z, row + 1 : row + 1 + ROWS, :]
            ahead_y = pltpu.roll(here, ny - 1, 1)
            if it == 0:
                old_z = start_p[0, z, row : row + ROWS, :]
                old_x = start_p[1, z, row : row + ROWS, :]
                old_y = start_p[2, z, row : row + ROWS, :]
                current = here
            else:
                old_z = dual_z[it - 1, z + 1, row : row + ROWS, :]
                old_x = dual_x[it - 1, z, ROWS + row : ROWS + row + ROWS, :]
                old_y = dual_y[it - 1, z, row : row + ROWS, :]
                current = value[it - 1, z, row : row + ROWS, :]
            moved_z = old_z + (0.25 * inside_z) * (ahead_z - here)
            moved_x = old_x + (0.25 * inside_x) * (ahead_x - here)
            moved_y = old_y + (0.25 * inside_y) * (ahead_y - here)
            size = moved_z * moved_z + moved_x * moved_x + moved_y * moved_y
            scale = lax.rsqrt(jnp.maximum(size, 1.0))
            new_y = moved_y * (scale * inside_y)
            dual_z[it, z + 1, row : row + ROWS, :] = moved_z * (scale * inside_z)
            dual_x[it, z, ROWS + row : ROWS + row + ROWS, :] = moved_x * (scale * inside_x)
            dual_y[it, z, row : row + ROWS, :] = new_y
            part[z, row : row + ROWS, :] = current + 0.25 * (new_y - pltpu.roll(new_y, 1, 1))
            return carry

        lax.fori_loop(low, high, body, 0)

    def over(low, high, body):
        def step(z, carry):
            for c in range(chunks):
                body(z, pl.ds(c * chunk, chunk))
            return carry

        lax.fori_loop(low, high, step, 0)

    def add_votes(k, z, rows, lanes, sums):
        shift = (slab * nz + z).astype(jnp.float32) * (UNIT / BAND)
        for view in range(VIEWS):
            reach = jnp.maximum(batch[k, view, rows, lanes] - shift, 0.0)
            clipped = [jnp.minimum(reach, UNIT + 0.1 * i) for i in range(BINS)]
            sums = clipped if sums is None else [s + c for s, c in zip(sums, clipped)]
        return sums

    def field_pass(it, group, low, high):
        row = ROWS * group
        rows = pl.ds(row, ROWS)

        def body(z, lanes):
            if it == 0:
                sums = add_votes(0, z, rows, lanes, None)
                for i in range(BINS):
                    votes[i, z, rows, lanes] = sums[i]
            else:
                before = [votes[i, z, rows, lanes] for i in range(BINS)]
                sums = add_votes(1, z, rows, lanes, before)
            moved = dual_z[it, z + 1, rows, lanes] - dual_z[it, z, rows, lanes]
            moved = moved + (
                dual_x[it, z, pl.ds(ROWS + row, ROWS), lanes]
                - dual_x[it, z, pl.ds(ROWS + row - 1, ROWS), lanes]
            )
            values = part[z, rows, lanes] + 0.25 * moved
            total = sums[0] * (0.05 / UNIT)
            base = values - total
            best = jnp.maximum(base, jnp.minimum(values + total, -1.0))
            for i in range(1, BINS):
                centre = -1.0 + 2.0 * i / (BINS - 1)
                best = jnp.maximum(
                    best, jnp.minimum(base + (sums[i] - sums[i - 1]), centre)
                )
            if it == ITERS - 1:
                field_out[z, rows, lanes] = best
            else:
                value[it, z, rows, lanes] = best
                extra[1, z, rows, lanes] = 2.0 * best - extra[0, z, rows, lanes]

        over(low, high, body)

    first_copy(0).start()
    into_field.wait()
    pack_extra(0)
    into_owner.wait()
    into_visible.wait()
    pass_on(0, 0)
    send_halo(0, 0)
    send_halo(0, 1)
    first_copy(1).start()
    into_dual.wait()
    for group in range(groups - 1):
        dual_pass(0, group, 0, nz - 1)
    for stage in range(1, last - 1):
        pass_on(0, stage)
    take_halo(0, 0)
    take_halo(0, 1)
    for group in range(groups):
        dual_pass(0, group, nz - 1, nz)
    send_halo(0, 2)
    dual_pass(0, groups - 1, 0, nz - 1)
    pack_dual(0)
    send_halo(0, 3)
    pass_on(1, 0)
    if last > 1:
        pass_on(0, last - 1)
    take_halo(0, 2)
    take_halo(0, 3)
    last_copy(0).wait_recv()

    for group in range(groups):
        field_pass(0, group, 0, 1)
    send_halo(1, 0)
    for stage in range(1, last - 1):
        pass_on(1, stage)
    field_pass(0, 0, 1, nz)
    pack_extra(1)
    send_halo(1, 1)
    for group in range(1, groups):
        field_pass(0, group, 1, nz)
    if last > 1:
        pass_on(1, last - 1)
    for group in range(groups - 1):
        dual_pass(1, group, 0, nz - 1)
    take_halo(1, 0)
    take_halo(1, 1)
    for group in range(groups):
        dual_pass(1, group, nz - 1, nz)
    send_halo(1, 2)
    dual_pass(1, groups - 1, 0, nz - 1)
    pack_dual(1)
    send_halo(1, 3)
    out_dual = [
        pltpu.make_async_copy(
            dual_z.at[1, pl.ds(1, nz)], dual_out.at[0], local_sem.at[4]
        ),
        pltpu.make_async_copy(
            dual_x.at[1, pl.ds(0, nz), pl.ds(ROWS, nx)], dual_out.at[1], local_sem.at[5]
        ),
        pltpu.make_async_copy(dual_y.at[1], dual_out.at[2], local_sem.at[6]),
    ]
    for copy in out_dual:
        copy.start()
    last_copy(1).wait_recv()
    for group in range(1, groups):
        field_pass(1, group, 1, nz)
    take_halo(1, 2)
    take_halo(1, 3)
    for group in range(groups):
        field_pass(1, group, 0, 1)
    field_pass(1, 0, 1, nz)

    for k in range(ITERS):
        first_copy(k).wait_send()
        for stage in range(1, last):
            for piece in range(2):
                middle_copy(k, stage, piece).wait_send()
        last_copy(k).wait_send()
    for it in range(ITERS):
        for kind in range(4):
            sent_halo(it, kind)
    for copy in out_dual:
        copy.wait()


def write_out(field_kept, dual_kept, field_out, dual_out, sem):
    copies = [pltpu.make_async_copy(field_kept, field_out, sem.at[3])]
    for c in range(3):
        copies.append(pltpu.make_async_copy(dual_kept.at[c], dual_out.at[c], sem.at[c]))
    for copy in copies:
        copy.start()
    for copy in copies:
        copy.wait()


def per_device(n_slab, n_tile, field, dual, depth, owner, visible):
    nz, nx, ny = field.shape
    stages = 1
    while 2**stages < n_slab:
        stages += 1
    slots = stages + 1
    f32 = jnp.float32
    anywhere = pl.BlockSpec(memory_space=pl.ANY)
    field_kept, dual_kept = pl.pallas_call(
        functools.partial(kernel, n_slab, n_tile),
        out_shape=(
            pltpu.VMEM(field.shape, f32),
            pltpu.VMEM(dual.shape, f32),
        ),
        in_specs=[anywhere] * 5,
        out_specs=(pl.BlockSpec(memory_space=pltpu.VMEM),) * 2,
        scratch_shapes=[
            pltpu.VMEM((ITERS, nz + 1, nx + 8, ny), f32),
            pltpu.VMEM((3, nz, nx, ny), f32),
            pltpu.VMEM((ITERS, nz + 1, nx, ny), f32),
            pltpu.VMEM((ITERS, nz, nx + 8, ny), f32),
            pltpu.VMEM((ITERS, nz, nx, ny), f32),
            pltpu.VMEM((nz, nx, ny), f32),
            pltpu.VMEM((ITERS, nz, nx, ny), f32),
            pltpu.VMEM((BINS, nz, nx, ny), f32),
            pltpu.VMEM((ITERS, HALF, nx, ny), f32),
            pltpu.VMEM((ITERS, slots, HALF, nx, ny), f32),
            pltpu.VMEM((ITERS, slots, HALF, nx, ny), f32),
            pltpu.VMEM((ITERS, VIEWS, nx, ny), f32),
            pltpu.VMEM((ITERS, 2, nz, ny), f32),
            pltpu.VMEM((ITERS, 2, nz, ny), f32),
            pltpu.SemaphoreType.DMA((ITERS, slots, 2)),
            pltpu.SemaphoreType.DMA((ITERS, slots, 2)),
            pltpu.SemaphoreType.DMA((ITERS, 4)),
            pltpu.SemaphoreType.DMA((ITERS, 4)),
            pltpu.SemaphoreType.DMA((10,)),
            pltpu.SMEM(owner.shape, jnp.int32),
            pltpu.SMEM((ITERS, 1, VIEWS), jnp.int32),
        ],
        compiler_params=pltpu.CompilerParams(
            collective_id=0, has_side_effects=True, vmem_limit_bytes=VMEM - 4 * (field.size + dual.size)
        ),
        name="merge",
    )(owner, jnp.swapaxes(visible, 1, 2), field, dual, depth)
    return pl.pallas_call(
        write_out,
        out_shape=(
            jax.ShapeDtypeStruct(field.shape, f32),
            jax.ShapeDtypeStruct(dual.shape, f32),
        ),
        in_specs=[pl.BlockSpec(memory_space=pltpu.VMEM)] * 2,
        out_specs=(anywhere, anywhere),
        scratch_shapes=[pltpu.SemaphoreType.DMA((4,))],
        compiler_params=pltpu.CompilerParams(vmem_limit_bytes=4 * 2**20),
        name="write",
    )(field_kept, dual_kept)


def solution(mesh):
    placed = (
        P("slab", "tile", None),
        P(None, "slab", "tile", None),
        P("slab", None, None, "tile", None),
        P(),
        P(None, None, "tile"),
    )
    return jax.shard_map(
        functools.partial(per_device, mesh.shape["slab"], mesh.shape["tile"]),
        mesh=mesh,
        in_specs=placed,
        out_specs=(P("slab", "tile", None), P(None, "slab", "tile", None)),
        check_vma=False,
    )
```
